768 devices in a mesh: rows: 24 (over y_lo, z), cells: 32 (over x, y_hi, core).
Axes of the slice: x: 4, y: 8 (y_hi: 4, y_lo: 2; y = y_hi * 2 + y_lo), z: 12, core: 2. Of those that a mesh axis runs over, the one named last changes fastest.
Arguments:
- tiles: bfloat16 [24, 32, 8, 512, 512], P('rows', 'cells'), may hold values from -0.0625 to 0.0625
- tile_rows: int32 [24, 32, 8], P('rows', 'cells'), may hold values from 0 to 7, as said below
- tile_cols: int32 [24, 32, 8], P('rows', 'cells'), may hold values from 0 to 7
- tile_count: int32 [24, 32], P('rows', 'cells'), may hold values from 2 to 8, as said below
- probes: bfloat16 [16, 131072], P(None, 'cells'), may hold values from -6 to 6
- noise_weight: float32 [98304], P('rows'), may hold values from 0.2 to 5
Outputs:
- hess_probes: float32 [16, 131072], P(None, 'cells')
The draws below stay inside these ranges and needn't reach their ends.
Inputs may be any that keep to these rules, and one draw needn't show every extreme that they name: `tile_rows`: within one device the used slots name distinct (row block, cell block) pairs. `tile_count`: some device uses all 8 slots.
All inputs are finite; a program needn't handle non-finite values.
Results may differ from the reference program's by a relative error of at most 0.0025.
Values may be sent and summed in bfloat16 or wider, within the bound.
No kernel may reach another device: no remote copies, remote signals or barrier semaphores. Data moves between devices by JAX's collectives and lax.ppermute only.
A program may use at most 32 MiB of HBM per device.

```python
import math
import jax
import jax.numpy as jnp
from jax import lax

TILE = 512
PROBES = 16
RB = 8
CB = 8
TILES_DEV = 8
RGROUPS = 24
CGROUPS = 32
DATA = 98304
CELLS = 131072
N_CELLS = 32


def tile_pairs(key):
    keys = jax.random.split(key, RGROUPS * CGROUPS)
    picked = jax.vmap(lambda single: jax.random.permutation(single, RB * CB)[:TILES_DEV])(keys)
    return picked.reshape(RGROUPS, CGROUPS, TILES_DEV).astype(jnp.int32)


def draw_tile_rows(key, part):
    pairs = tile_pairs(key)
    return (pairs // CB).astype(jnp.int32)


def draw_tile_cols(key, part):
    pairs = tile_pairs(key)
    return (pairs % CB).astype(jnp.int32)


def draw_tile_count(key, part):
    key = jax.random.fold_in(key, 3)
    lowest = max(1, TILES_DEV // 4)
    counts = jax.random.randint(key, (RGROUPS * CGROUPS,), lowest, TILES_DEV + 1).astype(jnp.int32)
    places = jax.random.permutation(jax.random.fold_in(key, 5), RGROUPS * CGROUPS)
    counts = counts.at[places[0]].set(TILES_DEV).at[places[1]].set(lowest)
    return counts.reshape(RGROUPS, CGROUPS).astype(jnp.int32)


def block_levels(stream_key, dims, cuts, low, top_value):
    gain = 1.0
    for position, shards_of in cuts:
        draws = jax.random.uniform(jax.random.fold_in(jax.random.fold_in(stream_key, 6), position), (shards_of,), jnp.float32, low / len(cuts), top_value / len(cuts))
        gain = gain * jnp.repeat(jnp.exp(draws), dims[position] // shards_of).reshape((-1,) + (1,) * (len(dims) - 1 - position))
    return gain


def scatter_about(rng, extent, spread, reach, cuts=(), kind=jnp.bfloat16):
    array = jax.random.normal(rng, extent, jnp.float32) * spread
    if len(cuts) > 0:
        array = block_levels(rng, extent, cuts, -0.22, 0.18) * array
    return jnp.clip(array, min=-reach, max=reach).astype(kind)


def setup_inputs(seed: int = 0) -> dict:
    seeds = jax.random.split(jax.random.key(seed), 7)
    tiles = scatter_about(seeds[0], (RGROUPS, CGROUPS, TILES_DEV, TILE, TILE), (TILE * N_CELLS * TILES_DEV // RB // 2) ** -0.5, 0.0625, ((0, 24), (1, 32)))
    tile_rows = draw_tile_rows(jax.random.fold_in(seeds[6], 71), 0)
    tile_cols = draw_tile_cols(jax.random.fold_in(seeds[6], 71), 0)
    tile_count = draw_tile_count(jax.random.fold_in(seeds[6], 71), 0)
    probes = scatter_about(seeds[4], (PROBES, CELLS), 1.0, 6.0, ((1, 32),))
    noise_weight = jnp.clip(jnp.exp(math.log(5.0) - 3.218876 * jax.random.uniform(seeds[5], (DATA,), jnp.float32) ** block_levels(seeds[5], (DATA,), ((0, 24),), -0.2, 0.2)), 0.2, 5.0)
    return dict(tiles=tiles, tile_rows=tile_rows, tile_cols=tile_cols, tile_count=tile_count, probes=probes, noise_weight=noise_weight)


def reference(tiles, tile_rows, tile_cols, tile_count, probes, noise_weight):
    groups_r = tiles.shape[0]
    groups_c = tiles.shape[1]
    slots = tiles.shape[2]
    width = tiles.shape[3]
    flat_tiles = tiles.reshape(groups_r * groups_c * slots, width, width)
    rgrid = jnp.arange(groups_r, dtype=jnp.int32)[:, None, None] + jnp.zeros((groups_r, groups_c, slots), jnp.int32)
    cgrid = jnp.arange(groups_c, dtype=jnp.int32)[None, :, None] + jnp.zeros((groups_r, groups_c, slots), jnp.int32)
    kgrid = jnp.arange(slots, dtype=jnp.int32)[None, None, :] + jnp.zeros((groups_r, groups_c, slots), jnp.int32)
    used = (kgrid < tile_count[:, :, None]).reshape(-1)
    row_start = ((rgrid * RB + tile_rows) * width).reshape(-1).astype(jnp.int32)
    col_start = ((cgrid * CB + tile_cols) * width).reshape(-1).astype(jnp.int32)
    nprobe = probes.shape[0]

    def forward(acc, item):
        tile, flag, rstart, cstart = item
        source = lax.dynamic_slice_in_dim(probes, cstart, width, 1)
        part = lax.dot_general(source, tile, (((1,), (1,)), ((), ())), preferred_element_type=jnp.float32)
        part = jnp.where(flag, part, jnp.zeros_like(part))
        current = lax.dynamic_slice_in_dim(acc, rstart, width, 1)
        return lax.dynamic_update_slice_in_dim(acc, current + part, rstart, 1), None

    predicted, _ = lax.scan(forward, jnp.zeros((nprobe, noise_weight.shape[0]), jnp.float32), (flat_tiles, used, row_start, col_start))
    weighted = (noise_weight[None, :] * predicted).astype(jnp.bfloat16)

    def backward(acc, item):
        tile, flag, rstart, cstart = item
        source = lax.dynamic_slice_in_dim(weighted, rstart, width, 1)
        part = jnp.dot(source, tile, preferred_element_type=jnp.float32)
        part = jnp.where(flag, part, jnp.zeros_like(part))
        current = lax.dynamic_slice_in_dim(acc, cstart, width, 1)
        return lax.dynamic_update_slice_in_dim(acc, current + part, cstart, 1), None

    result, _ = lax.scan(backward, jnp.zeros((nprobe, probes.shape[1]), jnp.float32), (flat_tiles, used, row_start, col_start))
    return result
```

```python
import jax
import jax.numpy as jnp
from jax import lax
from jax.experimental import pallas as pl
from jax.experimental.pallas import tpu as pltpu
from jax.sharding import PartitionSpec as P

LANES = 128
SUB = 8
SMEM = pl.BlockSpec(memory_space=pltpu.SMEM)
VMEM = pl.BlockSpec(memory_space=pltpu.VMEM)
ANY = pl.BlockSpec(memory_space=pl.ANY)


def load_tiles(count_ref, tiles_ref, held, sems):
    used = count_ref[0, 0]

    def copy(slot):
        return pltpu.make_async_copy(tiles_ref.at[0, 0, slot], held.at[slot], sems.at[slot])

    def start(slot, carry):
        copy(slot).start()
        return carry

    lax.fori_loop(0, used, start, 0)
    return used, lambda slot: copy(slot).wait()


def forward_kernel(rows_ref, cols_ref, count_ref, probes_ref, tiles_ref, out_ref, held, sems):
    width = held.shape[1]
    per = width // LANES
    used, wait = load_tiles(count_ref, tiles_ref, held, sems)
    out_ref[...] = jnp.zeros_like(out_ref)

    def step(slot, carry):
        row = rows_ref[0, 0, slot]
        col = cols_ref[0, 0, slot]
        source = probes_ref[:, pl.ds(pl.multiple_of(col * width, width), width)]
        wait(slot)
        part = lax.dot_general(
            source, held[slot], (((1,), (1,)), ((), ())), preferred_element_type=jnp.float32
        )
        for q in range(per):
            out_ref[row * per + q] += part[:, q * LANES : (q + 1) * LANES]
        return carry

    lax.fori_loop(0, used, step, 0)


def weight_kernel(got_ref, noise_ref, out_ref):
    total = jnp.sum(got_ref[...], axis=0)
    weighted = (noise_ref[...] * total).astype(out_ref.dtype)
    out_ref[...] = jnp.broadcast_to(weighted[None], out_ref.shape)


def backward_kernel(rows_ref, cols_ref, count_ref, weighted_ref, tiles_ref, out_ref, held, sems):
    width = held.shape[1]
    per = width // LANES
    nprobe = weighted_ref.shape[1]
    halves = nprobe // SUB
    chunks = weighted_ref.shape[0]
    used, wait = load_tiles(count_ref, tiles_ref, held, sems)
    out_ref[...] = jnp.zeros_like(out_ref)

    def step(slot, carry):
        row = rows_ref[0, 0, slot]
        col = cols_ref[0, 0, slot]
        source = jnp.concatenate([weighted_ref[row * per + q] for q in range(per)], axis=1)
        wait(slot)
        part = jnp.dot(source, held[slot], preferred_element_type=jnp.float32)
        for h in range(halves):
            for q in range(per):
                out_ref[h * chunks + col * per + q] += part[
                    h * SUB : (h + 1) * SUB, q * LANES : (q + 1) * LANES
                ]
        return carry

    lax.fori_loop(0, used, step, 0)


def total_kernel(got_ref, out_ref):
    out_ref[...] = jnp.broadcast_to(jnp.sum(got_ref[...], axis=0)[None], out_ref.shape)


def solution(mesh):
    nrows = mesh.shape["rows"]
    ncells = mesh.shape["cells"]

    def shards(tiles, tile_rows, tile_cols, tile_count, probes, noise_weight):
        slots, width = tiles.shape[2], tiles.shape[3]
        nprobe, ncell = probes.shape
        ndata = noise_weight.shape[0]
        halves = nprobe // SUB
        chunks = ndata // LANES
        blocks = halves * (ncell // LANES)
        share = -(-blocks // nrows)
        scratch = [
            pltpu.VMEM((slots, width, width), tiles.dtype),
            pltpu.SemaphoreType.DMA((slots,)),
        ]
        params = pltpu.CompilerParams(vmem_limit_bytes=16 << 20)

        partial = pl.pallas_call(
            forward_kernel,
            out_shape=jax.ShapeDtypeStruct((chunks, nprobe, LANES), jnp.float32),
            in_specs=[SMEM, SMEM, SMEM, VMEM, ANY],
            out_specs=VMEM,
            scratch_shapes=scratch,
            compiler_params=params,
        )(tile_rows, tile_cols, tile_count, probes, tiles)
        got = lax.all_to_all(partial, "cells", 0, 0, tiled=True)

        noise = lax.dynamic_slice_in_dim(
            noise_weight, lax.axis_index("cells") * LANES, LANES, 0
        ).reshape(1, LANES)
        weighted = pl.pallas_call(
            weight_kernel,
            out_shape=jax.ShapeDtypeStruct((ncells, nprobe, LANES), jnp.bfloat16),
            in_specs=[VMEM, VMEM],
            out_specs=VMEM,
        )(got, noise)
        weighted = lax.all_to_all(weighted, "cells", 0, 0, tiled=True)

        product = pl.pallas_call(
            backward_kernel,
            out_shape=jax.ShapeDtypeStruct((nrows * share, SUB, LANES), jnp.float32),
            in_specs=[SMEM, SMEM, SMEM, VMEM, ANY],
            out_specs=VMEM,
            scratch_shapes=scratch,
            compiler_params=params,
        )(tile_rows, tile_cols, tile_count, weighted, tiles)
        got = lax.all_to_all(product, "rows", 0, 0, tiled=True)

        total = pl.pallas_call(
            total_kernel,
            out_shape=jax.ShapeDtypeStruct((nrows, share, SUB, LANES), jnp.float32),
            in_specs=[VMEM],
            out_specs=VMEM,
        )(got.reshape(nrows, share, SUB, LANES))
        full = lax.all_to_all(
            total.reshape(nrows * share, SUB, LANES), "rows", 0, 0, tiled=True
        )
        full = full[:blocks].reshape(halves, ncell // LANES, SUB, LANES)
        return full.transpose(0, 2, 1, 3).reshape(nprobe, ncell)

    in_specs = (
        P("rows", "cells", None, None, None),
        P("rows", "cells", None),
        P("rows", "cells", None),
        P("rows", "cells"),
        P(None, "cells"),
        P("rows"),
    )
    return jax.shard_map(
        shards, mesh=mesh, in_specs=in_specs, out_specs=P(None, "cells"), check_vma=False
    )
```

```python
import jax
import jax.numpy as jnp
from jax import lax
from jax.experimental import pallas as pl
from jax.experimental.pallas import tpu as pltpu
from jax.sharding import PartitionSpec as P

LANES = 128
SUB = 8
SMEM = pl.BlockSpec(memory_space=pltpu.SMEM)
VMEM = pl.BlockSpec(memory_space=pltpu.VMEM)
HBM = pl.BlockSpec(memory_space=pltpu.HBM)


def in_hbm(array):
    return pltpu.with_memory_space_constraint(array, pltpu.HBM)


def forward_kernel(
    rows_hbm, cols_hbm, count_ref, noise_hbm, probes_hbm, tiles_hbm,
    out_ref, noise_ref, held_ref,
    rows_ref, cols_ref, probes_ref, small_sems, tile_sems,
):
    slots, width = held_ref.shape[0], held_ref.shape[1]
    per = width // LANES
    mine = lax.axis_index("cells")

    def tile_copy(slot):
        return pltpu.make_async_copy(tiles_hbm.at[0, 0, slot], held_ref.at[slot], tile_sems.at[slot])

    first = [
        pltpu.make_async_copy(rows_hbm, rows_ref, small_sems.at[0]),
        pltpu.make_async_copy(cols_hbm, cols_ref, small_sems.at[1]),
        pltpu.make_async_copy(probes_hbm, probes_ref, small_sems.at[2]),
    ]
    noise_copy = pltpu.make_async_copy(noise_hbm.at[pl.ds(mine, 1)], noise_ref, small_sems.at[3])
    for copy in first:
        copy.start()
    for slot in range(slots):
        tile_copy(slot).start()
    noise_copy.start()
    out_ref[...] = jnp.zeros_like(out_ref)
    for copy in first:
        copy.wait()
    used = count_ref[0, 0]

    def step(slot, carry):
        row = rows_ref[0, 0, slot]
        col = cols_ref[0, 0, slot]
        source = probes_ref[:, pl.ds(pl.multiple_of(col * width, width), width)]
        tile_copy(slot).wait()
        part = lax.dot_general(
            source, held_ref[slot], (((1,), (1,)), ((), ())), preferred_element_type=jnp.float32
        )
        for q in range(per):
            out_ref[row * per + q] += part[:, q * LANES : (q + 1) * LANES]
        return carry

    def drain(slot, carry):
        tile_copy(slot).wait()
        return carry

    lax.fori_loop(0, used, step, 0)
    lax.fori_loop(used, slots, drain, 0)
    noise_copy.wait()


def backward_kernel(rows_ref, cols_ref, count_ref, weighted_ref, held_ref, out_ref):
    width = held_ref.shape[1]
    per = width // LANES
    chunks, nprobe, _ = weighted_ref.shape
    halves = nprobe // SUB
    out_ref[...] = jnp.zeros_like(out_ref)

    def step(slot, carry):
        row = rows_ref[0, 0, slot]
        col = cols_ref[0, 0, slot]
        source = jnp.concatenate([weighted_ref[row * per + q] for q in range(per)], axis=1)
        part = jnp.dot(source, held_ref[slot], preferred_element_type=jnp.float32)
        for h in range(halves):
            for q in range(per):
                out_ref[h * chunks + col * per + q] += part[
                    h * SUB : (h + 1) * SUB, q * LANES : (q + 1) * LANES
                ]
        return carry

    lax.fori_loop(0, count_ref[0, 0], step, 0)


def solution(mesh):
    nrows = mesh.shape["rows"]
    ncells = mesh.shape["cells"]

    def shards(tiles, tile_rows, tile_cols, tile_count, probes, noise_weight):
        slots, width = tiles.shape[2], tiles.shape[3]
        nprobe, ncell = probes.shape
        ndata = noise_weight.shape[0]
        halves = nprobe // SUB
        chunks = ndata // LANES
        blocks = halves * (ncell // LANES)
        share = -(-blocks // nrows)
        params = pltpu.CompilerParams(vmem_limit_bytes=16 << 20)

        partial, noise, held = pl.pallas_call(
            forward_kernel,
            out_shape=(
                jax.ShapeDtypeStruct((chunks, nprobe, LANES), jnp.float32),
                jax.ShapeDtypeStruct((1, LANES), jnp.float32),
                jax.ShapeDtypeStruct((slots, width, width), tiles.dtype),
            ),
            in_specs=[HBM, HBM, SMEM, HBM, HBM, HBM],
            out_specs=(VMEM, VMEM, VMEM),
            scratch_shapes=[
                pltpu.SMEM(tile_rows.shape, tile_rows.dtype),
                pltpu.SMEM(tile_cols.shape, tile_cols.dtype),
                pltpu.VMEM(probes.shape, probes.dtype),
                pltpu.SemaphoreType.DMA((4,)),
                pltpu.SemaphoreType.DMA((slots,)),
            ],
            compiler_params=params,
        )(
            in_hbm(tile_rows), in_hbm(tile_cols), tile_count,
            in_hbm(noise_weight.reshape(chunks, LANES)), in_hbm(probes), in_hbm(tiles),
        )

        got = lax.all_to_all(partial, "cells", 0, 0, tiled=True)
        weighted = (noise * jnp.sum(got, axis=0)).astype(jnp.bfloat16)
        weighted = lax.all_to_all(
            jnp.broadcast_to(weighted[None], (ncells, nprobe, LANES)), "cells", 0, 0, tiled=True
        )

        product = pl.pallas_call(
            backward_kernel,
            out_shape=jax.ShapeDtypeStruct((nrows * share, SUB, LANES), jnp.float32),
            in_specs=[SMEM, SMEM, SMEM, VMEM, VMEM],
            out_specs=VMEM,
            compiler_params=params,
        )(tile_rows, tile_cols, tile_count, weighted, held)

        got = lax.all_to_all(product, "rows", 0, 0, tiled=True)
        total = jnp.sum(got.reshape(nrows, share, SUB, LANES), axis=0)
        full = lax.all_to_all(
            jnp.broadcast_to(total[None], (nrows, share, SUB, LANES)).reshape(-1, SUB, LANES),
            "rows", 0, 0, tiled=True,
        )
        full = full[:blocks].reshape(halves, ncell // LANES, SUB, LANES)
        return full.transpose(0, 2, 1, 3).reshape(nprobe, ncell)

    in_specs = (
        P("rows", "cells", None, None, None),
        P("rows", "cells", None),
        P("rows", "cells", None),
        P("rows", "cells"),
        P(None, "cells"),
        P("rows"),
    )
    return jax.shard_map(
        shards, mesh=mesh, in_specs=in_specs, out_specs=P(None, "cells"), check_vma=False
    )
```

```python
import jax
import jax.numpy as jnp
from jax import lax
from jax.experimental import pallas as pl
from jax.experimental.pallas import tpu as pltpu
from jax.sharding import PartitionSpec as P

LANES = 128
SUB = 8
SMEM = pl.BlockSpec(memory_space=pltpu.SMEM)
VMEM = pl.BlockSpec(memory_space=pltpu.VMEM)
HBM = pl.BlockSpec(memory_space=pltpu.HBM)


def in_hbm(array):
    return pltpu.with_memory_space_constraint(array, pltpu.HBM)


def forward_kernel(
    rows_hbm, cols_hbm, count_ref, noise_hbm, probes_hbm, tiles_hbm,
    out_ref, noise_ref,
    rows_ref, cols_ref, probes_ref, held_ref, small_sems, tile_sems,
):
    slots, width = held_ref.shape[0], held_ref.shape[1]
    per = width // LANES
    mine = lax.axis_index("cells")

    def tile_copy(slot):
        return pltpu.make_async_copy(tiles_hbm.at[0, 0, slot], held_ref.at[slot], tile_sems.at[slot])

    first = [
        pltpu.make_async_copy(rows_hbm, rows_ref, small_sems.at[0]),
        pltpu.make_async_copy(cols_hbm, cols_ref, small_sems.at[1]),
        pltpu.make_async_copy(probes_hbm, probes_ref, small_sems.at[2]),
    ]
    noise_copy = pltpu.make_async_copy(noise_hbm.at[pl.ds(mine, 1)], noise_ref, small_sems.at[3])
    for copy in first:
        copy.start()
    for slot in range(slots):
        tile_copy(slot).start()
    noise_copy.start()
    out_ref[...] = jnp.zeros_like(out_ref)
    for copy in first:
        copy.wait()
    used = count_ref[0, 0]

    def step(slot, carry):
        row = rows_ref[0, 0, slot]
        col = cols_ref[0, 0, slot]
        source = probes_ref[:, pl.ds(pl.multiple_of(col * width, width), width)]
        tile_copy(slot).wait()
        part = lax.dot_general(
            source, held_ref[slot], (((1,), (1,)), ((), ())), preferred_element_type=jnp.float32
        )
        for q in range(per):
            out_ref[row * per + q] += part[:, q * LANES : (q + 1) * LANES]
        return carry

    def drain(slot, carry):
        tile_copy(slot).wait()
        return carry

    lax.fori_loop(0, used, step, 0)
    lax.fori_loop(used, slots, drain, 0)
    noise_copy.wait()


def backward_kernel(
    rows_ref, cols_ref, count_ref, weighted_ref, tiles_hbm, out_ref, held_ref, tile_sems
):
    slots = held_ref.shape[0]
    width = held_ref.shape[1]
    per = width // LANES
    chunks, nprobe, _ = weighted_ref.shape
    halves = nprobe // SUB

    def tile_copy(slot):
        return pltpu.make_async_copy(tiles_hbm.at[0, 0, slot], held_ref.at[slot], tile_sems.at[slot])

    for slot in range(slots):
        tile_copy(slot).start()
    used = count_ref[0, 0]
    out_ref[...] = jnp.zeros_like(out_ref)

    def step(slot, carry):
        row = rows_ref[0, 0, slot]
        col = cols_ref[0, 0, slot]
        source = jnp.concatenate([weighted_ref[row * per + q] for q in range(per)], axis=1)
        tile_copy(slot).wait()
        part = jnp.dot(source, held_ref[slot], preferred_element_type=jnp.float32)
        for h in range(halves):
            for q in range(per):
                out_ref[h * chunks + col * per + q] += part[
                    h * SUB : (h + 1) * SUB, q * LANES : (q + 1) * LANES
                ]
        return carry

    def drain(slot, carry):
        tile_copy(slot).wait()
        return carry

    lax.fori_loop(0, used, step, 0)
    lax.fori_loop(used, slots, drain, 0)


def solution(mesh):
    nrows = mesh.shape["rows"]
    ncells = mesh.shape["cells"]

    def shards(tiles, tile_rows, tile_cols, tile_count, probes, noise_weight):
        slots, width = tiles.shape[2], tiles.shape[3]
        nprobe, ncell = probes.shape
        ndata = noise_weight.shape[0]
        halves = nprobe // SUB
        chunks = ndata // LANES
        blocks = halves * (ncell // LANES)
        share = -(-blocks // nrows)
        params = pltpu.CompilerParams(vmem_limit_bytes=16 << 20)

        partial, noise = pl.pallas_call(
            forward_kernel,
            out_shape=(
                jax.ShapeDtypeStruct((chunks, nprobe, LANES), jnp.float32),
                jax.ShapeDtypeStruct((1, LANES), jnp.float32),
            ),
            in_specs=[HBM, HBM, SMEM, HBM, HBM, HBM],
            out_specs=(VMEM, VMEM),
            scratch_shapes=[
                pltpu.SMEM(tile_rows.shape, tile_rows.dtype),
                pltpu.SMEM(tile_cols.shape, tile_cols.dtype),
                pltpu.VMEM(probes.shape, probes.dtype),
                pltpu.VMEM((slots, width, width), tiles.dtype),
                pltpu.SemaphoreType.DMA((4,)),
                pltpu.SemaphoreType.DMA((slots,)),
            ],
            compiler_params=params,
        )(
            in_hbm(tile_rows), in_hbm(tile_cols), tile_count,
            in_hbm(noise_weight.reshape(chunks, LANES)), in_hbm(probes), in_hbm(tiles),
        )

        got = lax.all_to_all(partial, "cells", 0, 0, tiled=True)
        weighted = (noise * jnp.sum(got, axis=0)).astype(jnp.bfloat16)
        weighted = lax.all_to_all(
            jnp.broadcast_to(weighted[None], (ncells, nprobe, LANES)), "cells", 0, 0, tiled=True
        )

        product = pl.pallas_call(
            backward_kernel,
            out_shape=jax.ShapeDtypeStruct((nrows * share, SUB, LANES), jnp.float32),
            in_specs=[SMEM, SMEM, SMEM, VMEM, HBM],
            out_specs=VMEM,
            scratch_shapes=[
                pltpu.VMEM((slots, width, width), tiles.dtype),
                pltpu.SemaphoreType.DMA((slots,)),
            ],
            compiler_params=params,
        )(tile_rows, tile_cols, tile_count, weighted, in_hbm(tiles))

        got = lax.all_to_all(product.astype(jnp.bfloat16), "rows", 0, 0, tiled=True)
        total = jnp.sum(
            got.reshape(nrows, share, SUB, LANES).astype(jnp.float32), axis=0
        ).astype(jnp.bfloat16)
        full = lax.all_to_all(
            jnp.broadcast_to(total[None], (nrows, share, SUB, LANES)).reshape(-1, SUB, LANES),
            "rows", 0, 0, tiled=True,
        )
        full = full[:blocks].astype(jnp.float32).reshape(halves, ncell // LANES, SUB, LANES)
        return full.transpose(0, 2, 1, 3).reshape(nprobe, ncell)

    in_specs = (
        P("rows", "cells", None, None, None),
        P("rows", "cells", None),
        P("rows", "cells", None),
        P("rows", "cells"),
        P(None, "cells"),
        P("rows"),
    )
    return jax.shard_map(
        shards, mesh=mesh, in_specs=in_specs, out_specs=P(None, "cells"), check_vma=False
    )
```

```python
import jax
import jax.numpy as jnp
import numpy as np
from jax import lax
from jax.experimental import pallas as pl
from jax.experimental.pallas import tpu as pltpu
from jax.sharding import PartitionSpec as P

LANES = 128
SUB = 8
FAR = 4
CORES = 2
SMEM = pl.BlockSpec(memory_space=pltpu.SMEM)
VMEM = pl.BlockSpec(memory_space=pltpu.VMEM)
HBM = pl.BlockSpec(memory_space=pltpu.HBM)


def in_hbm(array):
    return pltpu.with_memory_space_constraint(array, pltpu.HBM)


def forward_kernel(
    rows_hbm, cols_hbm, count_ref, noise_hbm, probes_hbm, tiles_hbm,
    out_ref, noise_ref,
    rows_ref, cols_ref, probes_ref, held_ref, small_sems, tile_sems,
):
    slots, width = held_ref.shape[0], held_ref.shape[1]
    per = width // LANES
    mine = lax.axis_index("cells")
    place = mine // (FAR * CORES) * CORES + mine % CORES

    def tile_copy(slot):
        return pltpu.make_async_copy(tiles_hbm.at[0, 0, slot], held_ref.at[slot], tile_sems.at[slot])

    first = [
        pltpu.make_async_copy(rows_hbm, rows_ref, small_sems.at[0]),
        pltpu.make_async_copy(cols_hbm, cols_ref, small_sems.at[1]),
        pltpu.make_async_copy(probes_hbm, probes_ref, small_sems.at[2]),
    ]
    noise_copy = pltpu.make_async_copy(noise_hbm.at[place], noise_ref, small_sems.at[3])
    for copy in first:
        copy.start()
    for slot in range(slots):
        tile_copy(slot).start()
    noise_copy.start()
    out_ref[...] = jnp.zeros_like(out_ref)
    for copy in first:
        copy.wait()
    used = count_ref[0, 0]

    def step(slot, carry):
        row = rows_ref[0, 0, slot]
        col = cols_ref[0, 0, slot]
        source = probes_ref[:, pl.ds(pl.multiple_of(col * width, width), width)]
        tile_copy(slot).wait()
        part = lax.dot_general(
            source, held_ref[slot], (((1,), (1,)), ((), ())), preferred_element_type=jnp.float32
        )
        for q in range(per):
            out_ref[row * per + q] += part[:, q * LANES : (q + 1) * LANES]
        return carry

    def drain(slot, carry):
        tile_copy(slot).wait()
        return carry

    lax.fori_loop(0, used, step, 0)
    lax.fori_loop(used, slots, drain, 0)
    noise_copy.wait()


def backward_kernel(
    rows_ref, cols_ref, count_ref, weighted_ref, tiles_hbm, out_ref, held_ref, tile_sems
):
    slots = held_ref.shape[0]
    width = held_ref.shape[1]
    per = width // LANES
    chunks, nprobe, _ = weighted_ref.shape
    halves = nprobe // SUB

    def tile_copy(slot):
        return pltpu.make_async_copy(tiles_hbm.at[0, 0, slot], held_ref.at[slot], tile_sems.at[slot])

    for slot in range(slots):
        tile_copy(slot).start()
    used = count_ref[0, 0]
    out_ref[...] = jnp.zeros_like(out_ref)

    def step(slot, carry):
        row = rows_ref[0, 0, slot]
        col = cols_ref[0, 0, slot]
        source = jnp.concatenate([weighted_ref[row * per + q] for q in range(per)], axis=1)
        tile_copy(slot).wait()
        part = jnp.dot(source, held_ref[slot], preferred_element_type=jnp.float32)
        for h in range(halves):
            for q in range(per):
                out_ref[h * chunks + col * per + q] += part[
                    h * SUB : (h + 1) * SUB, q * LANES : (q + 1) * LANES
                ]
        return carry

    def drain(slot, carry):
        tile_copy(slot).wait()
        return carry

    lax.fori_loop(0, used, step, 0)
    lax.fori_loop(used, slots, drain, 0)


def solution(mesh):
    nrows = mesh.shape["rows"]
    ncells = mesh.shape["cells"]
    near = ncells // FAR
    grid = np.arange(ncells).reshape(-1, FAR, CORES)
    near_groups = grid.transpose(1, 0, 2).reshape(FAR, near).tolist()
    far_groups = grid.transpose(0, 2, 1).reshape(near, FAR).tolist()

    def shards(tiles, tile_rows, tile_cols, tile_count, probes, noise_weight):
        slots, width = tiles.shape[2], tiles.shape[3]
        nprobe, ncell = probes.shape
        ndata = noise_weight.shape[0]
        halves = nprobe // SUB
        chunks = ndata // LANES
        blocks = halves * (ncell // LANES)
        share = -(-blocks // nrows)
        params = pltpu.CompilerParams(vmem_limit_bytes=16 << 20)

        partial, noise = pl.pallas_call(
            forward_kernel,
            out_shape=(
                jax.ShapeDtypeStruct((chunks, nprobe, LANES), jnp.float32),
                jax.ShapeDtypeStruct((chunks // near, LANES), jnp.float32),
            ),
            in_specs=[HBM, HBM, SMEM, HBM, HBM, HBM],
            out_specs=(VMEM, VMEM),
            scratch_shapes=[
                pltpu.SMEM(tile_rows.shape, tile_rows.dtype),
                pltpu.SMEM(tile_cols.shape, tile_cols.dtype),
                pltpu.VMEM(probes.shape, probes.dtype),
                pltpu.VMEM((slots, width, width), tiles.dtype),
                pltpu.SemaphoreType.DMA((4,)),
                pltpu.SemaphoreType.DMA((slots,)),
            ],
            compiler_params=params,
        )(
            in_hbm(tile_rows), in_hbm(tile_cols), tile_count,
            in_hbm(noise_weight.reshape(near, chunks // near, LANES)), in_hbm(probes), in_hbm(tiles),
        )

        part = chunks // near
        got = lax.all_to_all(partial, "cells", 0, 0, axis_index_groups=near_groups, tiled=True)
        near_sum = jnp.sum(got.reshape(near, part, nprobe, LANES), axis=0)
        got = lax.all_to_all(
            jnp.broadcast_to(near_sum[None], (FAR, part, nprobe, LANES)),
            "cells", 0, 0, axis_index_groups=far_groups, tiled=True,
        )
        weighted = (noise[:, None, :] * jnp.sum(got, axis=0)).astype(jnp.bfloat16)
        weighted = lax.all_to_all(
            jnp.broadcast_to(weighted[None], (near, part, nprobe, LANES)),
            "cells", 0, 0, axis_index_groups=near_groups, tiled=True,
        ).reshape(chunks, nprobe, LANES)

        product = pl.pallas_call(
            backward_kernel,
            out_shape=jax.ShapeDtypeStruct((nrows * share, SUB, LANES), jnp.float32),
            in_specs=[SMEM, SMEM, SMEM, VMEM, HBM],
            out_specs=VMEM,
            scratch_shapes=[
                pltpu.VMEM((slots, width, width), tiles.dtype),
                pltpu.SemaphoreType.DMA((slots,)),
            ],
            compiler_params=params,
        )(tile_rows, tile_cols, tile_count, weighted, in_hbm(tiles))

        got = lax.all_to_all(product.astype(jnp.bfloat16), "rows", 0, 0, tiled=True)
        total = jnp.sum(
            got.reshape(nrows, share, SUB, LANES).astype(jnp.float32), axis=0
        ).astype(jnp.bfloat16)
        full = lax.all_to_all(
            jnp.broadcast_to(total[None], (nrows, share, SUB, LANES)).reshape(-1, SUB, LANES),
            "rows", 0, 0, tiled=True,
        )
        full = full[:blocks].astype(jnp.float32).reshape(halves, ncell // LANES, SUB, LANES)
        return full.transpose(0, 2, 1, 3).reshape(nprobe, ncell)

    in_specs = (
        P("rows", "cells", None, None, None),
        P("rows", "cells", None),
        P("rows", "cells", None),
        P("rows", "cells"),
        P(None, "cells"),
        P("rows"),
    )
    return jax.shard_map(
        shards, mesh=mesh, in_specs=in_specs, out_specs=P(None, "cells"), check_vma=False
    )
```

```python
import jax
import jax.numpy as jnp
import numpy as np
from jax import lax
from jax.experimental import pallas as pl
from jax.experimental.pallas import tpu as pltpu
from jax.sharding import PartitionSpec as P

LANES = 128
SUB = 8
KEEP = 6
FAR = 4
CORES = 2
SMEM = pl.BlockSpec(memory_space=pltpu.SMEM)
VMEM = pl.BlockSpec(memory_space=pltpu.VMEM)
HBM = pl.BlockSpec(memory_space=pltpu.HBM)


def in_hbm(array):
    return pltpu.with_memory_space_constraint(array, pltpu.HBM)


def small_copies(pairs, sems):
    return [pltpu.make_async_copy(hbm, ref, sems.at[n]) for n, (hbm, ref) in enumerate(pairs)]


def in_pairs(used, slots, waits, product):
    steps = (used + 1) // 2
    for part, (first, last) in enumerate(((0, KEEP), (KEEP, slots))):
        begin, end = first // 2, last // 2
        middle = jnp.clip(steps, begin, end)

        def step(pair, carry, part=part):
            one, two = 2 * pair, 2 * pair + 1
            waits[part](one)
            waits[part](two)
            last_used = jnp.minimum(two, used - 1)
            product[part](one, two, last_used, two < used)
            return carry

        def drain(pair, carry, part=part):
            waits[part](2 * pair)
            waits[part](2 * pair + 1)
            return carry

        lax.fori_loop(begin, middle, step, 0)
        lax.fori_loop(middle, end, drain, 0)


def forward_kernel(
    rows_hbm, cols_hbm, count_ref, noise_hbm, probes_hbm, tiles_hbm,
    out_ref, noise_ref, kept_ref,
    rows_ref, cols_ref, probes_ref, held_ref, small_sems, noise_sem, tile_sems,
):
    slots, width = KEEP + held_ref.shape[0], held_ref.shape[1]
    per = width // LANES
    mine = lax.axis_index("cells")
    place = mine // (FAR * CORES) * CORES + mine % CORES

    def kept_copy(slot):
        return pltpu.make_async_copy(tiles_hbm.at[0, 0, slot], kept_ref.at[slot], tile_sems.at[slot])

    def held_copy(slot):
        return pltpu.make_async_copy(
            tiles_hbm.at[0, 0, slot], held_ref.at[slot - KEEP], tile_sems.at[slot]
        )

    first = small_copies(
        [(rows_hbm, rows_ref), (cols_hbm, cols_ref), (probes_hbm, probes_ref)],
        small_sems,
    )
    noise_copy = pltpu.make_async_copy(noise_hbm.at[place], noise_ref, noise_sem)
    for copy in first:
        copy.start()
    for slot in range(KEEP):
        kept_copy(slot).start()
    for slot in range(KEEP, slots):
        held_copy(slot).start()
    noise_copy.start()
    out_ref[...] = jnp.zeros_like(out_ref)
    for copy in first:
        copy.wait()

    def product(tile):
        def both(one, two, at_two, two_used):
            parts = []
            for slot, at in ((one, one), (two, at_two)):
                col = cols_ref[0, 0, at]
                source = probes_ref[:, pl.ds(pl.multiple_of(col * width, width), width)]
                parts.append(
                    lax.dot_general(
                        source, tile(slot), (((1,), (1,)), ((), ())),
                        preferred_element_type=jnp.float32,
                    )
                )
            parts[1] = jnp.where(two_used, parts[1], 0.0)
            for at, part in zip((one, at_two), parts):
                row = rows_ref[0, 0, at]
                for q in range(per):
                    out_ref[row * per + q] += part[:, q * LANES : (q + 1) * LANES]

        return both

    in_pairs(
        count_ref[0, 0], slots,
        (lambda slot: kept_copy(slot).wait(), lambda slot: held_copy(slot).wait()),
        (product(lambda slot: kept_ref[slot]), product(lambda slot: held_ref[slot - KEEP])),
    )
    noise_copy.wait()


def backward_kernel(
    rows_hbm, cols_hbm, count_ref, weighted_ref, kept_ref, tiles_hbm,
    out_ref,
    rows_ref, cols_ref, held_ref, small_sems, tile_sems,
):
    slots, width = KEEP + held_ref.shape[0], held_ref.shape[1]
    per = width // LANES
    chunks, nprobe, _ = weighted_ref.shape
    halves = nprobe // SUB

    def held_copy(slot):
        return pltpu.make_async_copy(
            tiles_hbm.at[0, 0, slot], held_ref.at[slot - KEEP], tile_sems.at[slot - KEEP]
        )

    first = small_copies([(rows_hbm, rows_ref), (cols_hbm, cols_ref)], small_sems)
    for copy in first:
        copy.start()
    for slot in range(KEEP, slots):
        held_copy(slot).start()
    out_ref[...] = jnp.zeros_like(out_ref)
    for copy in first:
        copy.wait()

    def product(tile):
        def both(one, two, at_two, two_used):
            parts = []
            for slot, at in ((one, one), (two, at_two)):
                row = rows_ref[0, 0, at]
                source = jnp.concatenate([weighted_ref[row * per + q] for q in range(per)], axis=1)
                parts.append(jnp.dot(source, tile(slot), preferred_element_type=jnp.float32))
            parts[1] = jnp.where(two_used, parts[1], 0.0)
            for at, part in zip((one, at_two), parts):
                col = cols_ref[0, 0, at]
                for h in range(halves):
                    for q in range(per):
                        out_ref[h * chunks + col * per + q] += part[
                            h * SUB : (h + 1) * SUB, q * LANES : (q + 1) * LANES
                        ]

        return both

    in_pairs(
        count_ref[0, 0], slots,
        (lambda slot: None, lambda slot: held_copy(slot).wait()),
        (product(lambda slot: kept_ref[slot]), product(lambda slot: held_ref[slot - KEEP])),
    )


def solution(mesh):
    nrows = mesh.shape["rows"]
    ncells = mesh.shape["cells"]
    near = ncells // FAR
    grid = np.arange(ncells).reshape(-1, FAR, CORES)
    near_groups = grid.transpose(1, 0, 2).reshape(FAR, near).tolist()
    far_groups = grid.transpose(0, 2, 1).reshape(near, FAR).tolist()

    def shards(tiles, tile_rows, tile_cols, tile_count, probes, noise_weight):
        slots, width = tiles.shape[2], tiles.shape[3]
        nprobe, ncell = probes.shape
        ndata = noise_weight.shape[0]
        halves = nprobe // SUB
        chunks = ndata // LANES
        blocks = halves * (ncell // LANES)
        share = -(-blocks // nrows)
        where = (in_hbm(tile_rows), in_hbm(tile_cols), tile_count)
        small = [pltpu.SMEM(array.shape, array.dtype) for array in (tile_rows, tile_cols)]
        params = pltpu.CompilerParams(vmem_limit_bytes=16 << 20)

        partial, noise, kept = pl.pallas_call(
            forward_kernel,
            out_shape=(
                jax.ShapeDtypeStruct((chunks, nprobe, LANES), jnp.float32),
                jax.ShapeDtypeStruct((chunks // near, LANES), jnp.float32),
                jax.ShapeDtypeStruct((KEEP, width, width), tiles.dtype),
            ),
            in_specs=[HBM, HBM, SMEM, HBM, HBM, HBM],
            out_specs=(VMEM, VMEM, VMEM),
            scratch_shapes=[
                *small,
                pltpu.VMEM(probes.shape, probes.dtype),
                pltpu.VMEM((slots - KEEP, width, width), tiles.dtype),
                pltpu.SemaphoreType.DMA((3,)),
                pltpu.SemaphoreType.DMA,
                pltpu.SemaphoreType.DMA((slots,)),
            ],
            compiler_params=params,
        )(
            *where, in_hbm(noise_weight.reshape(near, chunks // near, LANES)), in_hbm(probes), in_hbm(tiles)
        )

        part = chunks // near
        got = lax.all_to_all(partial, "cells", 0, 0, axis_index_groups=near_groups, tiled=True)
        near_sum = jnp.sum(got.reshape(near, part, nprobe, LANES), axis=0)
        got = lax.all_to_all(
            jnp.broadcast_to(near_sum[None], (FAR, part, nprobe, LANES)),
            "cells", 0, 0, axis_index_groups=far_groups, tiled=True,
        )
        weighted = (noise[:, None, :] * jnp.sum(got, axis=0)).astype(jnp.bfloat16)
        weighted = lax.all_to_all(
            jnp.broadcast_to(weighted[None], (near, part, nprobe, LANES)),
            "cells", 0, 0, axis_index_groups=near_groups, tiled=True,
        ).reshape(chunks, nprobe, LANES)

        product = pl.pallas_call(
            backward_kernel,
            out_shape=jax.ShapeDtypeStruct((nrows * share, SUB, LANES), jnp.float32),
            in_specs=[HBM, HBM, SMEM, VMEM, VMEM, HBM],
            out_specs=VMEM,
            scratch_shapes=[
                *small,
                pltpu.VMEM((slots - KEEP, width, width), tiles.dtype),
                pltpu.SemaphoreType.DMA((2,)),
                pltpu.SemaphoreType.DMA((slots - KEEP,)),
            ],
            compiler_params=params,
        )(*where, weighted, kept, in_hbm(tiles))

        got = lax.all_to_all(product.astype(jnp.bfloat16), "rows", 0, 0, tiled=True)
        total = jnp.sum(
            got.reshape(nrows, share, SUB, LANES).astype(jnp.float32), axis=0
        ).astype(jnp.bfloat16)
        full = lax.all_to_all(
            jnp.broadcast_to(total[None], (nrows, share, SUB, LANES)).reshape(-1, SUB, LANES),
            "rows", 0, 0, tiled=True,
        )
        full = full[:blocks].astype(jnp.float32).reshape(halves, ncell // LANES, SUB, LANES)
        return full.transpose(0, 2, 1, 3).reshape(nprobe, ncell)

    in_specs = (
        P("rows", "cells", None, None, None),
        P("rows", "cells", None),
        P("rows", "cells", None),
        P("rows", "cells"),
        P(None, "cells"),
        P("rows"),
    )
    return jax.shard_map(
        shards, mesh=mesh, in_specs=in_specs, out_specs=P(None, "cells"), check_vma=False
    )
```

```python
import jax
import jax.numpy as jnp
import numpy as np
from jax import lax
from jax.experimental import pallas as pl
from jax.experimental.pallas import tpu as pltpu
from jax.sharding import PartitionSpec as P

LANES = 128
SUB = 8
KEEP = 6
FAR = 4
CORES = 2
PAIR = 2
BLOCKS = 4
SMEM = pl.BlockSpec(memory_space=pltpu.SMEM)
VMEM = pl.BlockSpec(memory_space=pltpu.VMEM)
HBM = pl.BlockSpec(memory_space=pltpu.HBM)


def in_hbm(array):
    return pltpu.with_memory_space_constraint(array, pltpu.HBM)


def small_copies(pairs, sems):
    return [pltpu.make_async_copy(hbm, ref, sems.at[n]) for n, (hbm, ref) in enumerate(pairs)]


def in_pairs(used, slots, waits, product):
    steps = (used + 1) // 2
    for part, (first, last) in enumerate(((0, KEEP), (KEEP, slots))):
        begin, end = first // 2, last // 2
        middle = jnp.clip(steps, begin, end)

        def step(pair, carry, part=part):
            one, two = 2 * pair, 2 * pair + 1
            waits[part](one)
            waits[part](two)
            last_used = jnp.minimum(two, used - 1)
            product[part](one, two, last_used, two < used)
            return carry

        def drain(pair, carry, part=part):
            waits[part](2 * pair)
            waits[part](2 * pair + 1)
            return carry

        lax.fori_loop(begin, middle, step, 0)
        lax.fori_loop(middle, end, drain, 0)


def forward_kernel(
    rows_hbm, cols_hbm, count_ref, noise_hbm, probes_hbm, tiles_hbm,
    out_ref, noise_ref, kept_ref,
    rows_ref, cols_ref, probes_ref, held_ref, small_sems, noise_sem, tile_sems,
):
    slots, width = KEEP + held_ref.shape[0], held_ref.shape[1]
    per = width // LANES
    mine = lax.axis_index("cells")
    place = mine // (FAR * CORES) * CORES + mine % CORES

    def kept_copy(slot):
        return pltpu.make_async_copy(tiles_hbm.at[0, 0, slot], kept_ref.at[slot], tile_sems.at[slot])

    def held_copy(slot):
        return pltpu.make_async_copy(
            tiles_hbm.at[0, 0, slot], held_ref.at[slot - KEEP], tile_sems.at[slot]
        )

    first = small_copies(
        [(rows_hbm, rows_ref), (cols_hbm, cols_ref), (probes_hbm, probes_ref)],
        small_sems,
    )
    noise_copy = pltpu.make_async_copy(noise_hbm.at[place], noise_ref, noise_sem)
    for copy in first:
        copy.start()
    for slot in range(KEEP):
        kept_copy(slot).start()
    for slot in range(KEEP, slots):
        held_copy(slot).start()
    noise_copy.start()
    out_ref[...] = jnp.zeros_like(out_ref)
    for copy in first:
        copy.wait()

    def product(tile):
        def both(one, two, at_two, two_used):
            parts = []
            for slot, at in ((one, one), (two, at_two)):
                col = cols_ref[0, 0, at]
                source = probes_ref[:, pl.ds(pl.multiple_of(col * width, width), width)]
                parts.append(
                    lax.dot_general(
                        source, tile(slot), (((1,), (1,)), ((), ())),
                        preferred_element_type=jnp.float32,
                    )
                )
            parts[1] = jnp.where(two_used, parts[1], 0.0)
            for at, part in zip((one, at_two), parts):
                row = rows_ref[0, 0, at]
                for q in range(per):
                    out_ref[row * per + q] += part[:, q * LANES : (q + 1) * LANES]

        return both

    in_pairs(
        count_ref[0, 0], slots,
        (lambda slot: kept_copy(slot).wait(), lambda slot: held_copy(slot).wait()),
        (product(lambda slot: kept_ref[slot]), product(lambda slot: held_ref[slot - KEEP])),
    )
    noise_copy.wait()


def backward_kernel(
    rows_hbm, cols_hbm, count_ref, weighted_ref, kept_ref, tiles_hbm,
    out_ref,
    rows_ref, cols_ref, held_ref, small_sems, tile_sems,
):
    slots, width = KEEP + held_ref.shape[0], held_ref.shape[1]
    per = width // LANES
    chunks, nprobe, _ = weighted_ref.shape
    halves = nprobe // SUB

    def held_copy(slot):
        return pltpu.make_async_copy(
            tiles_hbm.at[0, 0, slot], held_ref.at[slot - KEEP], tile_sems.at[slot - KEEP]
        )

    first = small_copies([(rows_hbm, rows_ref), (cols_hbm, cols_ref)], small_sems)
    for copy in first:
        copy.start()
    for slot in range(KEEP, slots):
        held_copy(slot).start()
    out_ref[...] = jnp.zeros_like(out_ref)
    for copy in first:
        copy.wait()

    def product(tile):
        def both(one, two, at_two, two_used):
            parts = []
            for slot, at in ((one, one), (two, at_two)):
                row = rows_ref[0, 0, at]
                source = jnp.concatenate([weighted_ref[row * per + q] for q in range(per)], axis=1)
                parts.append(jnp.dot(source, tile(slot), preferred_element_type=jnp.float32))
            parts[1] = jnp.where(two_used, parts[1], 0.0)
            for at, part in zip((one, at_two), parts):
                col = cols_ref[0, 0, at]
                for h in range(halves):
                    for q in range(per):
                        out_ref[h * chunks + col * per + q] += part[
                            h * SUB : (h + 1) * SUB, q * LANES : (q + 1) * LANES
                        ]

        return both

    in_pairs(
        count_ref[0, 0], slots,
        (lambda slot: None, lambda slot: held_copy(slot).wait()),
        (product(lambda slot: kept_ref[slot]), product(lambda slot: held_ref[slot - KEEP])),
    )


def ring_pairs(rings):
    return [
        np.concatenate([rings[:, pair] for pair in pairs]).tolist()
        for pairs in (([0, 1], [2, 3]), ([1, 2], [0, 3]))
    ]


def pairwise_total(array, axis, steps):
    for pairs in steps:
        array = jnp.sum(lax.all_gather(array, axis, axis_index_groups=pairs), axis=0)
    return array


def solution(mesh):
    nrows = mesh.shape["rows"]
    ncells = mesh.shape["cells"]
    near = ncells // FAR
    grid = np.arange(ncells).reshape(-1, FAR, CORES)
    near_groups = grid.transpose(1, 0, 2).reshape(FAR, near).tolist()
    far_pairs = ring_pairs(grid.transpose(0, 2, 1).reshape(near, FAR))

    row_near = nrows // BLOCKS
    grid = np.arange(nrows).reshape(PAIR, BLOCKS, -1)
    row_near_groups = grid.transpose(1, 0, 2).reshape(BLOCKS, row_near).tolist()
    row_far_pairs = ring_pairs(grid.transpose(0, 2, 1).reshape(row_near, BLOCKS))

    def shards(tiles, tile_rows, tile_cols, tile_count, probes, noise_weight):
        slots, width = tiles.shape[2], tiles.shape[3]
        nprobe, ncell = probes.shape
        ndata = noise_weight.shape[0]
        halves = nprobe // SUB
        chunks = ndata // LANES
        blocks = halves * (ncell // LANES)
        share = -(-blocks // row_near)
        where = (in_hbm(tile_rows), in_hbm(tile_cols), tile_count)
        small = [pltpu.SMEM(array.shape, array.dtype) for array in (tile_rows, tile_cols)]
        params = pltpu.CompilerParams(vmem_limit_bytes=16 << 20)

        partial, noise, kept = pl.pallas_call(
            forward_kernel,
            out_shape=(
                jax.ShapeDtypeStruct((chunks, nprobe, LANES), jnp.float32),
                jax.ShapeDtypeStruct((chunks // near, LANES), jnp.float32),
                jax.ShapeDtypeStruct((KEEP, width, width), tiles.dtype),
            ),
            in_specs=[HBM, HBM, SMEM, HBM, HBM, HBM],
            out_specs=(VMEM, VMEM, VMEM),
            scratch_shapes=[
                *small,
                pltpu.VMEM(probes.shape, probes.dtype),
                pltpu.VMEM((slots - KEEP, width, width), tiles.dtype),
                pltpu.SemaphoreType.DMA((3,)),
                pltpu.SemaphoreType.DMA,
                pltpu.SemaphoreType.DMA((slots,)),
            ],
            compiler_params=params,
        )(
            *where, in_hbm(noise_weight.reshape(near, chunks // near, LANES)), in_hbm(probes), in_hbm(tiles)
        )

        part = chunks // near
        got = lax.all_to_all(partial, "cells", 0, 0, axis_index_groups=near_groups, tiled=True)
        near_sum = jnp.sum(got.reshape(near, part, nprobe, LANES), axis=0)
        total = pairwise_total(near_sum, "cells", far_pairs)
        weighted = (noise[:, None, :] * total).astype(jnp.bfloat16)
        weighted = lax.all_to_all(
            jnp.broadcast_to(weighted[None], (near, part, nprobe, LANES)),
            "cells", 0, 0, axis_index_groups=near_groups, tiled=True,
        ).reshape(chunks, nprobe, LANES)

        product = pl.pallas_call(
            backward_kernel,
            out_shape=jax.ShapeDtypeStruct((row_near * share, SUB, LANES), jnp.float32),
            in_specs=[HBM, HBM, SMEM, VMEM, VMEM, HBM],
            out_specs=VMEM,
            scratch_shapes=[
                *small,
                pltpu.VMEM((slots - KEEP, width, width), tiles.dtype),
                pltpu.SemaphoreType.DMA((2,)),
                pltpu.SemaphoreType.DMA((slots - KEEP,)),
            ],
            compiler_params=params,
        )(*where, weighted, kept, in_hbm(tiles))

        got = lax.all_to_all(
            product.astype(jnp.bfloat16), "rows", 0, 0, axis_index_groups=row_near_groups, tiled=True
        )
        total = jnp.sum(got.reshape(row_near, share, SUB, LANES).astype(jnp.float32), axis=0)
        total = pairwise_total(total, "rows", row_far_pairs).astype(jnp.bfloat16)
        full = lax.all_to_all(
            jnp.broadcast_to(total[None], (row_near, share, SUB, LANES)).reshape(-1, SUB, LANES),
            "rows", 0, 0, axis_index_groups=row_near_groups, tiled=True,
        )
        full = full[:blocks].astype(jnp.float32).reshape(halves, ncell // LANES, SUB, LANES)
        return full.transpose(0, 2, 1, 3).reshape(nprobe, ncell)

    in_specs = (
        P("rows", "cells", None, None, None),
        P("rows", "cells", None),
        P("rows", "cells", None),
        P("rows", "cells"),
        P(None, "cells"),
        P("rows"),
    )
    return jax.shard_map(
        shards, mesh=mesh, in_specs=in_specs, out_specs=P(None, "cells"), check_vma=False
    )
```

```python
import jax
import jax.numpy as jnp
import numpy as np
from jax import lax
from jax.experimental import pallas as pl
from jax.experimental.pallas import tpu as pltpu
from jax.sharding import PartitionSpec as P

LANES = 128
SUB = 8
KEEP = 6
FAR = 4
CORES = 2
PAIR = 2
BLOCKS = 4
SMEM = pl.BlockSpec(memory_space=pltpu.SMEM)
VMEM = pl.BlockSpec(memory_space=pltpu.VMEM)
HBM = pl.BlockSpec(memory_space=pltpu.HBM)


def in_hbm(array):
    return pltpu.with_memory_space_constraint(array, pltpu.HBM)


def small_copies(pairs, sems):
    return [pltpu.make_async_copy(hbm, ref, sems.at[n]) for n, (hbm, ref) in enumerate(pairs)]


def pair_copy(tiles_hbm, ref, sems, pair, first):
    return pltpu.make_async_copy(
        tiles_hbm.at[0, 0, pl.ds(2 * pair, 2)], ref.at[pl.ds(2 * (pair - first), 2)], sems.at[pair]
    )


def in_pairs(used, slots, waits, product):
    steps = (used + 1) // 2
    for part, (first, last) in enumerate(((0, KEEP), (KEEP, slots))):
        begin, end = first // 2, last // 2
        middle = jnp.clip(steps, begin, end)

        def step(pair, carry, part=part):
            one, two = 2 * pair, 2 * pair + 1
            waits[part](pair)
            last_used = jnp.minimum(two, used - 1)
            product[part](one, two, last_used, two < used)
            return carry

        def drain(pair, carry, part=part):
            waits[part](pair)
            return carry

        lax.fori_loop(begin, middle, step, 0)
        lax.fori_loop(middle, end, drain, 0)


def forward_kernel(
    rows_hbm, cols_hbm, count_ref, noise_hbm, probes_hbm, tiles_hbm,
    out_ref, noise_ref, kept_ref,
    rows_ref, cols_ref, probes_ref, held_ref, small_sems, noise_sem, tile_sems,
):
    slots, width = KEEP + held_ref.shape[0], held_ref.shape[1]
    per = width // LANES
    mine = lax.axis_index("cells")
    place = mine // (FAR * CORES) * CORES + mine % CORES

    def kept_copy(pair):
        return pair_copy(tiles_hbm, kept_ref, tile_sems, pair, 0)

    def held_copy(pair):
        return pair_copy(tiles_hbm, held_ref, tile_sems, pair, KEEP // 2)

    first = small_copies(
        [(rows_hbm, rows_ref), (cols_hbm, cols_ref), (probes_hbm, probes_ref)],
        small_sems,
    )
    noise_copy = pltpu.make_async_copy(noise_hbm.at[place], noise_ref, noise_sem)
    for copy in first:
        copy.start()
    for pair in range(KEEP // 2):
        kept_copy(pair).start()
    for pair in range(KEEP // 2, slots // 2):
        held_copy(pair).start()
    noise_copy.start()
    out_ref[...] = jnp.zeros_like(out_ref)
    for copy in first:
        copy.wait()

    def product(tile):
        def both(one, two, at_two, two_used):
            parts = []
            for slot, at in ((one, one), (two, at_two)):
                col = cols_ref[0, 0, at]
                source = probes_ref[:, pl.ds(pl.multiple_of(col * width, width), width)]
                parts.append(
                    lax.dot_general(
                        source, tile(slot), (((1,), (1,)), ((), ())),
                        preferred_element_type=jnp.float32,
                    )
                )
            parts[1] = jnp.where(two_used, parts[1], 0.0)
            for at, part in zip((one, at_two), parts):
                row = rows_ref[0, 0, at]
                for q in range(per):
                    out_ref[row * per + q] += part[:, q * LANES : (q + 1) * LANES]

        return both

    in_pairs(
        count_ref[0, 0], slots,
        (lambda pair: kept_copy(pair).wait(), lambda pair: held_copy(pair).wait()),
        (product(lambda slot: kept_ref[slot]), product(lambda slot: held_ref[slot - KEEP])),
    )
    noise_copy.wait()


def backward_kernel(
    rows_hbm, cols_hbm, count_ref, weighted_ref, kept_ref, tiles_hbm,
    out_ref,
    rows_ref, cols_ref, held_ref, small_sems, tile_sems,
):
    slots, width = KEEP + held_ref.shape[0], held_ref.shape[1]
    per = width // LANES
    chunks, nprobe, _ = weighted_ref.shape
    halves = nprobe // SUB

    def held_copy(pair):
        return pair_copy(tiles_hbm, held_ref, tile_sems, pair, KEEP // 2)

    first = small_copies([(rows_hbm, rows_ref), (cols_hbm, cols_ref)], small_sems)
    for copy in first:
        copy.start()
    for pair in range(KEEP // 2, slots // 2):
        held_copy(pair).start()
    out_ref[...] = jnp.zeros_like(out_ref)
    for copy in first:
        copy.wait()

    def product(tile):
        def both(one, two, at_two, two_used):
            parts = []
            for slot, at in ((one, one), (two, at_two)):
                row = rows_ref[0, 0, at]
                source = jnp.concatenate([weighted_ref[row * per + q] for q in range(per)], axis=1)
                parts.append(jnp.dot(source, tile(slot), preferred_element_type=jnp.float32))
            parts[1] = jnp.where(two_used, parts[1], 0.0)
            for at, part in zip((one, at_two), parts):
                col = cols_ref[0, 0, at]
                for h in range(halves):
                    for q in range(per):
                        out_ref[h * chunks + col * per + q] += part[
                            h * SUB : (h + 1) * SUB, q * LANES : (q + 1) * LANES
                        ]

        return both

    in_pairs(
        count_ref[0, 0], slots,
        (lambda pair: None, lambda pair: held_copy(pair).wait()),
        (product(lambda slot: kept_ref[slot]), product(lambda slot: held_ref[slot - KEEP])),
    )


def ring_pairs(rings):
    return [
        np.concatenate([rings[:, pair] for pair in pairs]).tolist()
        for pairs in (([0, 1], [2, 3]), ([1, 2], [0, 3]))
    ]


def pairwise_total(array, axis, steps):
    for pairs in steps:
        array = jnp.sum(lax.all_gather(array, axis, axis_index_groups=pairs), axis=0)
    return array


def solution(mesh):
    nrows = mesh.shape["rows"]
    ncells = mesh.shape["cells"]
    near = ncells // FAR
    grid = np.arange(ncells).reshape(-1, FAR, CORES)
    near_groups = grid.transpose(1, 0, 2).reshape(FAR, near).tolist()
    far_pairs = ring_pairs(grid.transpose(0, 2, 1).reshape(near, FAR))

    row_near = nrows // BLOCKS
    grid = np.arange(nrows).reshape(PAIR, BLOCKS, -1)
    row_near_groups = grid.transpose(1, 0, 2).reshape(BLOCKS, row_near).tolist()
    row_far_pairs = ring_pairs(grid.transpose(0, 2, 1).reshape(row_near, BLOCKS))

    def shards(tiles, tile_rows, tile_cols, tile_count, probes, noise_weight):
        slots, width = tiles.shape[2], tiles.shape[3]
        nprobe, ncell = probes.shape
        ndata = noise_weight.shape[0]
        halves = nprobe // SUB
        chunks = ndata // LANES
        blocks = halves * (ncell // LANES)
        share = -(-blocks // row_near)
        where = (in_hbm(tile_rows), in_hbm(tile_cols), tile_count)
        small = [pltpu.SMEM(array.shape, array.dtype) for array in (tile_rows, tile_cols)]
        params = pltpu.CompilerParams(vmem_limit_bytes=16 << 20)

        partial, noise, kept = pl.pallas_call(
            forward_kernel,
            out_shape=(
                jax.ShapeDtypeStruct((chunks, nprobe, LANES), jnp.float32),
                jax.ShapeDtypeStruct((chunks // near, LANES), jnp.float32),
                jax.ShapeDtypeStruct((KEEP, width, width), tiles.dtype),
            ),
            in_specs=[HBM, HBM, SMEM, HBM, HBM, HBM],
            out_specs=(VMEM, VMEM, VMEM),
            scratch_shapes=[
                *small,
                pltpu.VMEM(probes.shape, probes.dtype),
                pltpu.VMEM((slots - KEEP, width, width), tiles.dtype),
                pltpu.SemaphoreType.DMA((3,)),
                pltpu.SemaphoreType.DMA,
                pltpu.SemaphoreType.DMA((slots // 2,)),
            ],
            compiler_params=params,
        )(
            *where, in_hbm(noise_weight.reshape(near, chunks // near, LANES)), in_hbm(probes), in_hbm(tiles)
        )

        part = chunks // near
        got = lax.all_to_all(partial, "cells", 0, 0, axis_index_groups=near_groups, tiled=True)
        near_sum = jnp.sum(got.reshape(near, part, nprobe, LANES), axis=0)
        total = pairwise_total(near_sum, "cells", far_pairs)
        weighted = (noise[:, None, :] * total).astype(jnp.bfloat16)
        weighted = lax.all_to_all(
            jnp.broadcast_to(weighted[None], (near, part, nprobe, LANES)),
            "cells", 0, 0, axis_index_groups=near_groups, tiled=True,
        ).reshape(chunks, nprobe, LANES)

        product = pl.pallas_call(
            backward_kernel,
            out_shape=jax.ShapeDtypeStruct((row_near * share, SUB, LANES), jnp.float32),
            in_specs=[HBM, HBM, SMEM, VMEM, VMEM, HBM],
            out_specs=VMEM,
            scratch_shapes=[
                *small,
                pltpu.VMEM((slots - KEEP, width, width), tiles.dtype),
                pltpu.SemaphoreType.DMA((2,)),
                pltpu.SemaphoreType.DMA((slots // 2,)),
            ],
            compiler_params=params,
        )(*where, weighted, kept, in_hbm(tiles))

        got = lax.all_to_all(
            product.astype(jnp.bfloat16), "rows", 0, 0, axis_index_groups=row_near_groups, tiled=True
        )
        total = jnp.sum(got.reshape(row_near, share, SUB, LANES).astype(jnp.float32), axis=0)
        total = pairwise_total(total, "rows", row_far_pairs).astype(jnp.bfloat16)
        full = lax.all_to_all(
            jnp.broadcast_to(total[None], (row_near, share, SUB, LANES)).reshape(-1, SUB, LANES),
            "rows", 0, 0, axis_index_groups=row_near_groups, tiled=True,
        )
        full = full[:blocks].astype(jnp.float32).reshape(halves, ncell // LANES, SUB, LANES)
        return full.transpose(0, 2, 1, 3).reshape(nprobe, ncell)

    in_specs = (
        P("rows", "cells", None, None, None),
        P("rows", "cells", None),
        P("rows", "cells", None),
        P("rows", "cells"),
        P(None, "cells"),
        P("rows"),
    )
    return jax.shard_map(
        shards, mesh=mesh, in_specs=in_specs, out_specs=P(None, "cells"), check_vma=False
    )
```

```python
import jax
import jax.numpy as jnp
import numpy as np
from jax import lax
from jax.experimental import pallas as pl
from jax.experimental.pallas import tpu as pltpu
from jax.sharding import PartitionSpec as P

LANES = 128
SUB = 8
KEEP = 6
FAR = 4
CORES = 2
PAIR = 2
BLOCKS = 4
SMEM = pl.BlockSpec(memory_space=pltpu.SMEM)
VMEM = pl.BlockSpec(memory_space=pltpu.VMEM)
HBM = pl.BlockSpec(memory_space=pltpu.HBM)


def in_hbm(array):
    return pltpu.with_memory_space_constraint(array, pltpu.HBM)


def small_copies(pairs, sems):
    return [pltpu.make_async_copy(hbm, ref, sems.at[n]) for n, (hbm, ref) in enumerate(pairs)]


def pair_copy(tiles_hbm, ref, sems, pair, first):
    return pltpu.make_async_copy(
        tiles_hbm.at[0, 0, pl.ds(2 * pair, 2)], ref.at[pl.ds(2 * (pair - first), 2)], sems.at[pair]
    )


def in_pairs(used, slots, waits, product):
    steps = (used + 1) // 2
    for part, (first, last) in enumerate(((0, KEEP), (KEEP, slots))):
        begin, end = first // 2, last // 2
        middle = jnp.clip(steps, begin, end)

        def step(pair, carry, part=part):
            one, two = 2 * pair, 2 * pair + 1
            waits[part](pair)
            last_used = jnp.minimum(two, used - 1)
            product[part](one, two, last_used, two < used)
            return carry

        def drain(pair, carry, part=part):
            waits[part](pair)
            return carry

        lax.fori_loop(begin, middle, step, 0)
        lax.fori_loop(middle, end, drain, 0)


def forward_kernel(
    rows_hbm, cols_hbm, count_ref, noise_hbm, probes_hbm, tiles_hbm,
    out_ref, noise_ref, kept_ref,
    rows_ref, cols_ref, probes_ref, held_ref, small_sems, noise_sem, tile_sems,
):
    slots, width = KEEP + held_ref.shape[0], held_ref.shape[1]
    per = width // LANES
    mine = lax.axis_index("cells")
    lines = noise_hbm.shape[0] // CORES
    place = mine % CORES * lines + mine // (FAR * CORES)

    def kept_copy(pair):
        return pair_copy(tiles_hbm, kept_ref, tile_sems, pair, 0)

    def held_copy(pair):
        return pair_copy(tiles_hbm, held_ref, tile_sems, pair, KEEP // 2)

    first = small_copies(
        [(rows_hbm, rows_ref), (cols_hbm, cols_ref), (probes_hbm, probes_ref)],
        small_sems,
    )
    noise_copy = pltpu.make_async_copy(noise_hbm.at[place], noise_ref, noise_sem)
    for copy in first:
        copy.start()
    for pair in range(KEEP // 2):
        kept_copy(pair).start()
    for pair in range(KEEP // 2, slots // 2):
        held_copy(pair).start()
    noise_copy.start()
    out_ref[...] = jnp.zeros_like(out_ref)
    for copy in first:
        copy.wait()

    def product(tile):
        def both(one, two, at_two, two_used):
            parts = []
            for slot, at in ((one, one), (two, at_two)):
                col = cols_ref[0, 0, at]
                source = probes_ref[:, pl.ds(pl.multiple_of(col * width, width), width)]
                parts.append(
                    lax.dot_general(
                        source, tile(slot), (((1,), (1,)), ((), ())),
                        preferred_element_type=jnp.float32,
                    )
                )
            parts[1] = jnp.where(two_used, parts[1], 0.0)
            for at, part in zip((one, at_two), parts):
                row = rows_ref[0, 0, at]
                for q in range(per):
                    out_ref[row * per + q] += part[:, q * LANES : (q + 1) * LANES]

        return both

    in_pairs(
        count_ref[0, 0], slots,
        (lambda pair: kept_copy(pair).wait(), lambda pair: held_copy(pair).wait()),
        (product(lambda slot: kept_ref[slot]), product(lambda slot: held_ref[slot - KEEP])),
    )
    noise_copy.wait()


def backward_kernel(
    rows_hbm, cols_hbm, count_ref, weighted_ref, kept_ref, tiles_hbm,
    out_ref,
    rows_ref, cols_ref, held_ref, small_sems, tile_sems,
):
    slots, width = KEEP + held_ref.shape[0], held_ref.shape[1]
    per = width // LANES
    chunks, nprobe, _ = weighted_ref.shape
    halves = nprobe // SUB

    def held_copy(pair):
        return pair_copy(tiles_hbm, held_ref, tile_sems, pair, KEEP // 2)

    first = small_copies([(rows_hbm, rows_ref), (cols_hbm, cols_ref)], small_sems)
    for copy in first:
        copy.start()
    for pair in range(KEEP // 2, slots // 2):
        held_copy(pair).start()
    out_ref[...] = jnp.zeros_like(out_ref)
    for copy in first:
        copy.wait()

    def product(tile):
        def both(one, two, at_two, two_used):
            parts = []
            for slot, at in ((one, one), (two, at_two)):
                row = rows_ref[0, 0, at]
                source = jnp.concatenate([weighted_ref[row * per + q] for q in range(per)], axis=1)
                parts.append(jnp.dot(source, tile(slot), preferred_element_type=jnp.float32))
            parts[1] = jnp.where(two_used, parts[1], 0.0)
            for at, part in zip((one, at_two), parts):
                col = cols_ref[0, 0, at]
                for h in range(halves):
                    for q in range(per):
                        out_ref[h * chunks + col * per + q] += part[
                            h * SUB : (h + 1) * SUB, q * LANES : (q + 1) * LANES
                        ]

        return both

    in_pairs(
        count_ref[0, 0], slots,
        (lambda pair: None, lambda pair: held_copy(pair).wait()),
        (product(lambda slot: kept_ref[slot]), product(lambda slot: held_ref[slot - KEEP])),
    )


def ring_pairs(rings):
    return [
        np.concatenate([rings[:, pair] for pair in pairs]).tolist()
        for pairs in (([0, 1], [2, 3]), ([1, 2], [0, 3]))
    ]


def pairwise_total(array, axis, steps):
    for pairs in steps:
        array = jnp.sum(lax.all_gather(array, axis, axis_index_groups=pairs), axis=0)
    return array


def solution(mesh):
    nrows = mesh.shape["rows"]
    ncells = mesh.shape["cells"]
    near = ncells // FAR
    grid = np.arange(ncells).reshape(-1, FAR, CORES)
    near_groups = grid.transpose(1, 2, 0).reshape(FAR, near).tolist()
    far_pairs = ring_pairs(grid.transpose(2, 0, 1).reshape(near, FAR))

    row_near = nrows // BLOCKS
    grid = np.arange(nrows).reshape(PAIR, BLOCKS, -1)
    row_near_groups = grid.transpose(1, 0, 2).reshape(BLOCKS, row_near).tolist()
    row_far_pairs = ring_pairs(grid.transpose(0, 2, 1).reshape(row_near, BLOCKS))[::-1]

    def shards(tiles, tile_rows, tile_cols, tile_count, probes, noise_weight):
        slots, width = tiles.shape[2], tiles.shape[3]
        nprobe, ncell = probes.shape
        ndata = noise_weight.shape[0]
        halves = nprobe // SUB
        chunks = ndata // LANES
        blocks = halves * (ncell // LANES)
        share = -(-blocks // row_near)
        where = (in_hbm(tile_rows), in_hbm(tile_cols), tile_count)
        small = [pltpu.SMEM(array.shape, array.dtype) for array in (tile_rows, tile_cols)]
        params = pltpu.CompilerParams(vmem_limit_bytes=16 << 20)

        partial, noise, kept = pl.pallas_call(
            forward_kernel,
            out_shape=(
                jax.ShapeDtypeStruct((chunks, nprobe, LANES), jnp.float32),
                jax.ShapeDtypeStruct((chunks // near, LANES), jnp.float32),
                jax.ShapeDtypeStruct((KEEP, width, width), tiles.dtype),
            ),
            in_specs=[HBM, HBM, SMEM, HBM, HBM, HBM],
            out_specs=(VMEM, VMEM, VMEM),
            scratch_shapes=[
                *small,
                pltpu.VMEM(probes.shape, probes.dtype),
                pltpu.VMEM((slots - KEEP, width, width), tiles.dtype),
                pltpu.SemaphoreType.DMA((3,)),
                pltpu.SemaphoreType.DMA,
                pltpu.SemaphoreType.DMA((slots // 2,)),
            ],
            compiler_params=params,
        )(
            *where, in_hbm(noise_weight.reshape(near, chunks // near, LANES)), in_hbm(probes), in_hbm(tiles)
        )

        part = chunks // near
        got = lax.all_to_all(partial, "cells", 0, 0, axis_index_groups=near_groups, tiled=True)
        near_sum = jnp.sum(got.reshape(near, part, nprobe, LANES), axis=0)
        total = pairwise_total(near_sum, "cells", far_pairs)
        weighted = (noise[:, None, :] * total).astype(jnp.bfloat16)
        weighted = lax.all_to_all(
            jnp.broadcast_to(weighted[None], (near, part, nprobe, LANES)),
            "cells", 0, 0, axis_index_groups=near_groups, tiled=True,
        ).reshape(chunks, nprobe, LANES)

        product = pl.pallas_call(
            backward_kernel,
            out_shape=jax.ShapeDtypeStruct((row_near * share, SUB, LANES), jnp.float32),
            in_specs=[HBM, HBM, SMEM, VMEM, VMEM, HBM],
            out_specs=VMEM,
            scratch_shapes=[
                *small,
                pltpu.VMEM((slots - KEEP, width, width), tiles.dtype),
                pltpu.SemaphoreType.DMA((2,)),
                pltpu.SemaphoreType.DMA((slots // 2,)),
            ],
            compiler_params=params,
        )(*where, weighted, kept, in_hbm(tiles))

        got = lax.all_to_all(
            product.astype(jnp.bfloat16), "rows", 0, 0, axis_index_groups=row_near_groups, tiled=True
        )
        total = jnp.sum(got.reshape(row_near, share, SUB, LANES).astype(jnp.float32), axis=0)
        total = pairwise_total(total, "rows", row_far_pairs).astype(jnp.bfloat16)
        full = lax.all_to_all(
            jnp.broadcast_to(total[None], (row_near, share, SUB, LANES)).reshape(-1, SUB, LANES),
            "rows", 0, 0, axis_index_groups=row_near_groups, tiled=True,
        )
        full = full[:blocks].astype(jnp.float32).reshape(halves, ncell // LANES, SUB, LANES)
        return full.transpose(0, 2, 1, 3).reshape(nprobe, ncell)

    in_specs = (
        P("rows", "cells", None, None, None),
        P("rows", "cells", None),
        P("rows", "cells", None),
        P("rows", "cells"),
        P(None, "cells"),
        P("rows"),
    )
    return jax.shard_map(
        shards, mesh=mesh, in_specs=in_specs, out_specs=P(None, "cells"), check_vma=False
    )
```

```python
import jax
import jax.numpy as jnp
import numpy as np
from jax import lax
from jax.experimental import pallas as pl
from jax.experimental.pallas import tpu as pltpu
from jax.sharding import PartitionSpec as P

LANES = 128
SUB = 8
KEEP = 6
FAR = 4
CORES = 2
PAIR = 2
BLOCKS = 4
SMEM = pl.BlockSpec(memory_space=pltpu.SMEM)
VMEM = pl.BlockSpec(memory_space=pltpu.VMEM)
HBM = pl.BlockSpec(memory_space=pltpu.HBM)


def in_hbm(array):
    return pltpu.with_memory_space_constraint(array, pltpu.HBM)


def small_copies(pairs, sems):
    return [pltpu.make_async_copy(hbm, ref, sems.at[n]) for n, (hbm, ref) in enumerate(pairs)]


def pair_copy(tiles_hbm, ref, sems, pair, first):
    return pltpu.make_async_copy(
        tiles_hbm.at[0, 0, pl.ds(2 * pair, 2)], ref.at[pl.ds(2 * (pair - first), 2)], sems.at[pair]
    )


def in_pairs(used, slots, waits, product):
    steps = (used + 1) // 2
    for part, (first, last) in enumerate(((0, KEEP), (KEEP, slots))):
        begin, end = first // 2, last // 2
        middle = jnp.clip(steps, begin, end)

        def step(pair, carry, part=part):
            one, two = 2 * pair, 2 * pair + 1
            waits[part](pair)
            last_used = jnp.minimum(two, used - 1)
            product[part](one, two, last_used, two < used)
            return carry

        def drain(pair, carry, part=part):
            waits[part](pair)
            return carry

        lax.fori_loop(begin, middle, step, 0)
        lax.fori_loop(middle, end, drain, 0)


def forward_kernel(
    rows_hbm, cols_hbm, count_ref, noise_hbm, probes_hbm, tiles_hbm,
    out_ref, noise_ref, kept_ref,
    rows_ref, cols_ref, probes_ref, held_ref, small_sems, noise_sem, tile_sems,
):
    slots, width = KEEP + held_ref.shape[0], held_ref.shape[1]
    per = width // LANES
    mine = lax.axis_index("cells")
    lines = noise_hbm.shape[0] // CORES
    place = mine % CORES * lines + mine // (FAR * CORES)

    def kept_copy(pair):
        return pair_copy(tiles_hbm, kept_ref, tile_sems, pair, 0)

    def held_copy(pair):
        return pair_copy(tiles_hbm, held_ref, tile_sems, pair, KEEP // 2)

    first = small_copies(
        [(rows_hbm, rows_ref), (cols_hbm, cols_ref), (probes_hbm, probes_ref)],
        small_sems,
    )
    noise_copy = pltpu.make_async_copy(noise_hbm.at[place], noise_ref, noise_sem)
    for copy in first:
        copy.start()
    for pair in range(KEEP // 2):
        kept_copy(pair).start()
    for pair in range(KEEP // 2, slots // 2):
        held_copy(pair).start()
    noise_copy.start()
    out_ref[...] = jnp.zeros_like(out_ref)
    for copy in first:
        copy.wait()

    def product(tile):
        def both(one, two, at_two, two_used):
            parts = []
            for slot, at in ((one, one), (two, at_two)):
                col = cols_ref[0, 0, at]
                source = probes_ref[:, pl.ds(pl.multiple_of(col * width, width), width)]
                parts.append(
                    lax.dot_general(
                        source, tile(slot), (((1,), (1,)), ((), ())),
                        preferred_element_type=jnp.float32,
                    )
                )
            parts[1] = jnp.where(two_used, parts[1], 0.0)
            for at, part in zip((one, at_two), parts):
                row = rows_ref[0, 0, at]
                for q in range(per):
                    out_ref[row * per + q] += part[:, q * LANES : (q + 1) * LANES]

        return both

    in_pairs(
        count_ref[0, 0], slots,
        (lambda pair: kept_copy(pair).wait(), lambda pair: held_copy(pair).wait()),
        (product(lambda slot: kept_ref[slot]), product(lambda slot: held_ref[slot - KEEP])),
    )
    noise_copy.wait()


def backward_kernel(
    rows_hbm, cols_hbm, count_ref, weighted_ref, kept_ref, tiles_hbm,
    out_ref,
    rows_ref, cols_ref, held_ref, small_sems, tile_sems,
):
    slots, width = KEEP + held_ref.shape[0], held_ref.shape[1]
    per = width // LANES
    chunks, nprobe, _ = weighted_ref.shape
    halves = nprobe // SUB

    def held_copy(pair):
        return pair_copy(tiles_hbm, held_ref, tile_sems, pair, KEEP // 2)

    first = small_copies([(rows_hbm, rows_ref), (cols_hbm, cols_ref)], small_sems)
    for copy in first:
        copy.start()
    for pair in range(KEEP // 2, slots // 2):
        held_copy(pair).start()
    out_ref[...] = jnp.zeros_like(out_ref)
    for copy in first:
        copy.wait()

    def product(tile):
        def both(one, two, at_two, two_used):
            parts = []
            for slot, at in ((one, one), (two, at_two)):
                row = rows_ref[0, 0, at]
                source = jnp.concatenate([weighted_ref[row * per + q] for q in range(per)], axis=1)
                parts.append(jnp.dot(source, tile(slot), preferred_element_type=jnp.float32))
            parts[1] = jnp.where(two_used, parts[1], 0.0)
            for at, part in zip((one, at_two), parts):
                col = cols_ref[0, 0, at]
                for h in range(halves):
                    for q in range(per):
                        out_ref[h * chunks + col * per + q] += part[
                            h * SUB : (h + 1) * SUB, q * LANES : (q + 1) * LANES
                        ]

        return both

    in_pairs(
        count_ref[0, 0], slots,
        (lambda pair: None, lambda pair: held_copy(pair).wait()),
        (product(lambda slot: kept_ref[slot]), product(lambda slot: held_ref[slot - KEEP])),
    )


def ring_pairs(rings):
    return [
        np.concatenate([rings[:, pair] for pair in pairs]).tolist()
        for pairs in (([0, 1], [2, 3]), ([1, 2], [0, 3]))
    ]


def pairwise_total(array, axis, steps):
    for pairs in steps:
        array = jnp.sum(lax.all_gather(array, axis, axis_index_groups=pairs), axis=0)
    return array


def solution(mesh):
    nrows = mesh.shape["rows"]
    ncells = mesh.shape["cells"]
    near = ncells // FAR
    grid = np.arange(ncells).reshape(-1, FAR, CORES)
    near_groups = grid.transpose(1, 2, 0).reshape(FAR, near).tolist()
    far_pairs = ring_pairs(grid.transpose(2, 0, 1).reshape(near, FAR))[::-1]

    row_near = nrows // BLOCKS
    grid = np.arange(nrows).reshape(PAIR, BLOCKS, -1)
    row_near_groups = grid.transpose(1, 0, 2).reshape(BLOCKS, row_near).tolist()
    row_far_pairs = ring_pairs(grid.transpose(0, 2, 1).reshape(row_near, BLOCKS))[::-1]

    def shards(tiles, tile_rows, tile_cols, tile_count, probes, noise_weight):
        slots, width = tiles.shape[2], tiles.shape[3]
        nprobe, ncell = probes.shape
        ndata = noise_weight.shape[0]
        halves = nprobe // SUB
        chunks = ndata // LANES
        blocks = halves * (ncell // LANES)
        share = -(-blocks // row_near)
        where = (in_hbm(tile_rows), in_hbm(tile_cols), tile_count)
        small = [pltpu.SMEM(array.shape, array.dtype) for array in (tile_rows, tile_cols)]
        params = pltpu.CompilerParams(vmem_limit_bytes=16 << 20)

        partial, noise, kept = pl.pallas_call(
            forward_kernel,
            out_shape=(
                jax.ShapeDtypeStruct((chunks, nprobe, LANES), jnp.float32),
                jax.ShapeDtypeStruct((chunks // near, LANES), jnp.float32),
                jax.ShapeDtypeStruct((KEEP, width, width), tiles.dtype),
            ),
            in_specs=[HBM, HBM, SMEM, HBM, HBM, HBM],
            out_specs=(VMEM, VMEM, VMEM),
            scratch_shapes=[
                *small,
                pltpu.VMEM(probes.shape, probes.dtype),
                pltpu.VMEM((slots - KEEP, width, width), tiles.dtype),
                pltpu.SemaphoreType.DMA((3,)),
                pltpu.SemaphoreType.DMA,
                pltpu.SemaphoreType.DMA((slots // 2,)),
            ],
            compiler_params=params,
        )(
            *where, in_hbm(noise_weight.reshape(near, chunks // near, LANES)), in_hbm(probes), in_hbm(tiles)
        )

        part = chunks // near
        got = lax.all_to_all(partial, "cells", 0, 0, axis_index_groups=near_groups, tiled=True)
        near_sum = jnp.sum(got.reshape(near, part, nprobe, LANES), axis=0)
        total = pairwise_total(near_sum, "cells", far_pairs)
        weighted = (noise[:, None, :] * total).astype(jnp.bfloat16)
        weighted = lax.all_to_all(
            jnp.broadcast_to(weighted[None], (near, part, nprobe, LANES)),
            "cells", 0, 0, axis_index_groups=near_groups, tiled=True,
        ).reshape(chunks, nprobe, LANES)

        product = pl.pallas_call(
            backward_kernel,
            out_shape=jax.ShapeDtypeStruct((row_near * share, SUB, LANES), jnp.float32),
            in_specs=[HBM, HBM, SMEM, VMEM, VMEM, HBM],
            out_specs=VMEM,
            scratch_shapes=[
                *small,
                pltpu.VMEM((slots - KEEP, width, width), tiles.dtype),
                pltpu.SemaphoreType.DMA((2,)),
                pltpu.SemaphoreType.DMA((slots // 2,)),
            ],
            compiler_params=params,
        )(*where, weighted, kept, in_hbm(tiles))

        got = lax.all_to_all(
            product.astype(jnp.bfloat16), "rows", 0, 0, axis_index_groups=row_near_groups, tiled=True
        )
        total = jnp.sum(got.reshape(row_near, share, SUB, LANES).astype(jnp.float32), axis=0)
        total = pairwise_total(total, "rows", row_far_pairs).astype(jnp.bfloat16)
        full = lax.all_to_all(
            jnp.broadcast_to(total[None], (row_near, share, SUB, LANES)).reshape(-1, SUB, LANES),
            "rows", 0, 0, axis_index_groups=row_near_groups, tiled=True,
        )
        full = full[:blocks].astype(jnp.float32).reshape(halves, ncell // LANES, SUB, LANES)
        return full.transpose(0, 2, 1, 3).reshape(nprobe, ncell)

    in_specs = (
        P("rows", "cells", None, None, None),
        P("rows", "cells", None),
        P("rows", "cells", None),
        P("rows", "cells"),
        P(None, "cells"),
        P("rows"),
    )
    return jax.shard_map(
        shards, mesh=mesh, in_specs=in_specs, out_specs=P(None, "cells"), check_vma=False
    )
```
